768 devices in a mesh: rep: 48 (over z, y_hi), exp: 16 (over y_lo, x, core).
Axes of the slice: x: 4, y: 8 (y_hi: 4, y_lo: 2; y = y_hi * 2 + y_lo), z: 12, core: 2. Of those that a mesh axis runs over, the one named last changes fastest.
Arguments:
- tokens: bfloat16 [2, 1024, 2048], P(None, 'exp'), may hold values from -6 to 6
- cotangent: bfloat16 [2, 1024, 2048], P(None, 'exp'), may hold values from -6 to 6
- expert_ids: int32 [2, 1024, 8], P(None, 'exp'), may hold values from 0 to 127, all different within a row; in each aligned block of 64 rows (0 to 63, 64 to 127, ..., all dimensions but the last counted through in order) at most 8 rows name the same one
- route_probs: bfloat16 [2, 1024, 8], P(None, 'exp'), may hold values from 0.019897461 to 0.5
- gate_weight: bfloat16 [16, 12288, 2048], P('exp', 'rep'), may hold values from -0.125 to 0.125
- up_weight: bfloat16 [16, 12288, 2048], P('exp', 'rep'), may hold values from -0.125 to 0.125
- down_weight: bfloat16 [16, 12288, 2048], P('exp', 'rep'), may hold values from -0.078125 to 0.078125
Outputs:
- grad_tokens: bfloat16 [2, 1024, 2048], P(None, 'exp')
- grad_probs: float32 [2, 1024, 8], P(None, 'exp')
- grad_down: bfloat16 [16, 12288, 2048], P('exp', 'rep')
The draws below stay inside these ranges and needn't reach their ends.
Inputs may be any that keep to these rules, and one draw needn't show every extreme that they name: `expert_ids`: A token's 8 ids differ. In each aligned block of 64 tokens of one micro-batch no expert is named more than 8 times, a bound that some block reaches.
All inputs are finite; a program needn't handle non-finite values.
Results may differ from the reference program's by a relative error of at most 0.0051.
Values may be sent and summed in bfloat16 or wider, within the bound.
A program may use at most 32 MiB of HBM per device.

```python
import math
import jax
import jax.numpy as jnp
import numpy as np
from jax import lax

D = 2048
FF = 1536
TOPK = 8
EXPERTS = 128
MICRO = 2
TOK_DEV = 64
CAP = 8
TOKENS = 1024
N_EXP = 16


def block_levels(rng, dims, pieces, smallest, high):
    def one(axis_at, parts):
        heights = jax.random.uniform(jax.random.fold_in(jax.random.fold_in(rng, 6), axis_at), (parts,), jnp.float32, smallest / len(pieces), high / len(pieces))
        return jnp.repeat(jnp.exp(heights), dims[axis_at] // parts).reshape((-1,) + (1,) * (len(dims) - axis_at - 1))

    gain = one(*pieces[0])
    for cut in pieces[1:]:
        gain = gain * one(*cut)
    return gain


def routed_block(stream_key, own, number, rows, amount, top, reach, slope):
    order = jax.random.permutation(stream_key, amount)
    heavy_load, usual = shares(amount, rows * top, reach, slope, True), shares(amount, rows * top, reach, slope, False)
    places = jnp.arange(amount)

    def named(tallies, turn):
        used = int((tallies > 0).sum())
        fixed = max(1, used // 4)
        passed = fixed + (places - fixed + turn * (used - fixed)) % max(1, amount - fixed)
        return jnp.zeros((amount,), jnp.int32).at[order[jnp.where(places < fixed, places, passed)]].set(jnp.asarray(tallies, jnp.int32))

    tallies = jnp.where(number % 4 == 0, named(heavy_load, number // 4), named(usual, number - number // 4 - 1))
    mixed = jax.random.permutation(jax.random.fold_in(own, 3), amount)
    source_of, receiver = mixed[0:amount // 2 * 2:2], mixed[1:amount // 2 * 2:2]
    margin = jnp.minimum(tallies[source_of] - 1, reach - tallies[receiver]) // 2
    margin = jnp.where((source_of == order[0]) | (receiver == order[0]) | (tallies[receiver] == 0), 0, jnp.maximum(margin, 0))
    passed = jax.random.randint(jax.random.fold_in(own, 4), (amount // 2,), 0, 1 << 20) % (margin + 1)
    tallies = tallies.at[source_of].add(-passed).at[receiver].add(passed)
    labels = jnp.searchsorted(jnp.cumsum(tallies), jnp.arange(rows * top), side="right").astype(jnp.int32)
    grid = labels.reshape(top, rows).T
    grid = grid[jax.random.permutation(jax.random.fold_in(own, 1), rows)]
    turn = jax.random.randint(jax.random.fold_in(own, 2), (rows, 1), 0, top)
    return jnp.take_along_axis(grid, (jnp.arange(top)[None, :] + turn) % top, axis=1)


def shares(number_of, total, limit, slope, full):
    loads = [(1 << 20) // math.isqrt(standing ** slope) + 1 for standing in range(1, number_of + 1)]
    largest = limit if full else min(limit, max(-(-total // number_of), total * loads[0] // sum(loads)))
    least = 1 if total - largest >= number_of - 1 else 0
    given, rest = [largest] + [least] * (number_of - 1), total - largest - least * (number_of - 1)
    while rest > 0:
        candidates = [i for i in range(1, number_of) if given[i] < largest] or [i for i in range(1, number_of) if given[i] < limit]
        whole, left = sum([loads[i] for i in candidates]), rest
        for i in candidates:
            addition = min(limit - given[i], max(1, left * loads[i] // whole), rest)
            given[i] = given[i] + addition
            rest = rest - addition
    return np.array(given)


def gaussian(key, shape, spread, limit, pieces=(), kind=jnp.bfloat16):
    array = spread * jax.random.normal(key, shape, jnp.float32)
    if pieces:
        array = array * block_levels(key, shape, pieces, -0.22, 0.18)
    return jnp.clip(array, -limit, limit).astype(kind)


def setup_inputs(seed: int = 0) -> dict:
    keys = jax.random.split(jax.random.key(seed), 8)
    tokens = gaussian(keys[0], (MICRO, TOKENS, D), 1.0, 6.0, ((1, 16),))
    cotangent = gaussian(keys[1], (MICRO, TOKENS, D), 1.0, 6.0, ((1, 16),))
    expert_ids_keys = jax.random.split(jax.random.fold_in(keys[2], 1), MICRO * TOKENS // TOK_DEV)
    expert_ids_turns = jax.random.permutation(jax.random.fold_in(keys[2], 3), MICRO * TOKENS // TOK_DEV)
    expert_ids = jax.vmap(lambda own, number: routed_block(jax.random.fold_in(keys[2], 2), own, number, TOK_DEV, EXPERTS, TOPK, CAP, 1))(expert_ids_keys, expert_ids_turns).reshape((MICRO, TOKENS, TOPK))
    route_probs = jnp.clip(jnp.exp(math.log(0.5) - 3.224016 * jax.random.uniform(keys[3], (MICRO, TOKENS, TOPK), jnp.float32) ** block_levels(keys[3], (MICRO, TOKENS, TOPK), ((1, 16),), -0.2, 0.2)), 0.019897461, 0.5).astype(jnp.bfloat16)
    gate_weight = gaussian(keys[4], (N_EXP, EXPERTS // N_EXP * FF, D), D ** -0.5, 0.125, ((0, 16), (1, 48)))
    up_weight = gaussian(keys[5], (N_EXP, EXPERTS // N_EXP * FF, D), D ** -0.5, 0.125, ((0, 16), (1, 48)))
    down_weight = gaussian(keys[6], (N_EXP, EXPERTS // N_EXP * FF, D), (4 * FF) ** -0.5, 0.078125, ((0, 16), (1, 48)))
    return {"tokens": tokens, "cotangent": cotangent, "expert_ids": expert_ids, "route_probs": route_probs, "gate_weight": gate_weight, "up_weight": up_weight, "down_weight": down_weight}


def slot_table(expert_ids):
    blocks = expert_ids.reshape(MICRO, N_EXP, TOK_DEV * TOPK)
    one_hot = (blocks[..., None] == jnp.arange(EXPERTS, dtype=jnp.int32)).astype(jnp.int32)
    before = jnp.cumsum(one_hot, axis=2) - one_hot
    slot_index = jnp.sum(before * one_hot, axis=-1).astype(jnp.int32)
    micro_index = jnp.broadcast_to(jnp.arange(MICRO, dtype=jnp.int32)[:, None, None], blocks.shape)
    group_index = jnp.broadcast_to(jnp.arange(N_EXP, dtype=jnp.int32)[None, :, None], blocks.shape)
    route_index = jnp.arange(MICRO * TOKENS * TOPK, dtype=jnp.int32).reshape(blocks.shape)
    owner = jnp.zeros((MICRO, N_EXP, EXPERTS, CAP), jnp.int32)
    owner = owner.at[micro_index, group_index, blocks, slot_index].set(route_index + 1)
    return owner


def reference(tokens, cotangent, expert_ids, route_probs, gate_weight, up_weight, down_weight):
    owner = slot_table(expert_ids)
    token_rows = tokens.reshape(MICRO * TOKENS, D)
    cot_rows = cotangent.reshape(MICRO * TOKENS, D)
    prob_flat = route_probs.reshape(MICRO * TOKENS * TOPK)
    gate_all = gate_weight.reshape(EXPERTS, FF, D)
    up_all = up_weight.reshape(EXPERTS, FF, D)
    down_all = down_weight.reshape(EXPERTS, FF, D)

    def per_expert(expert):
        routes = lax.dynamic_index_in_dim(owner, expert, 2, False).reshape(-1)
        valid = routes > 0
        route_idx = jnp.maximum(routes - 1, 0).astype(jnp.int32)
        token_idx = (route_idx // TOPK).astype(jnp.int32)
        x_rows = jnp.where(valid[:, None], token_rows[token_idx], jnp.zeros((), tokens.dtype))
        g_rows = jnp.where(valid[:, None], cot_rows[token_idx], jnp.zeros((), cotangent.dtype))
        probs = jnp.where(valid, prob_flat[route_idx].astype(jnp.float32), jnp.zeros((), jnp.float32))
        w_gate = gate_all[expert]
        w_upper = up_all[expert]
        w_lower = down_all[expert]
        gate_pre = jnp.dot(x_rows, w_gate.T, preferred_element_type=jnp.float32)
        up_pre = jnp.dot(x_rows, w_upper.T, preferred_element_type=jnp.float32)
        act_grad = jnp.dot(g_rows, w_lower.T, preferred_element_type=jnp.float32)
        sigmoid_gate = jax.nn.sigmoid(gate_pre)
        silu_gate = gate_pre * sigmoid_gate
        act = silu_gate * up_pre
        prob_grad = jnp.sum(act * act_grad, axis=-1)
        weighted_act = (probs[:, None] * act).astype(jnp.bfloat16)
        scaled = probs[:, None] * act_grad
        gate_grad = (scaled * up_pre * sigmoid_gate * (1.0 + gate_pre * (1.0 - sigmoid_gate))).astype(jnp.bfloat16)
        up_grad = (scaled * silu_gate).astype(jnp.bfloat16)
        route_grad = jnp.dot(gate_grad, w_gate, preferred_element_type=jnp.float32) + jnp.dot(up_grad, w_upper, preferred_element_type=jnp.float32)
        down_grad = jnp.dot(weighted_act.T, g_rows, preferred_element_type=jnp.float32).astype(jnp.bfloat16)
        return down_grad, route_grad, prob_grad, route_idx, valid

    down_grads, route_grads, prob_grads, route_ids, valids = lax.map(per_expert, jnp.arange(EXPERTS, dtype=jnp.int32))
    route_ids = route_ids.reshape(-1)
    valids = valids.reshape(-1)
    route_grads = jnp.where(valids[:, None], route_grads.reshape(-1, D), jnp.zeros((), jnp.float32))
    prob_grads = jnp.where(valids, prob_grads.reshape(-1), jnp.zeros((), jnp.float32))
    token_ids = (route_ids // TOPK).astype(jnp.int32)
    grad_rows = jnp.zeros((MICRO * TOKENS, D), jnp.float32).at[token_ids].add(route_grads)
    grad_prob_flat = jnp.zeros((MICRO * TOKENS * TOPK,), jnp.float32).at[route_ids].add(prob_grads)
    grad_tokens = grad_rows.reshape(MICRO, TOKENS, D).astype(jnp.bfloat16)
    grad_probs = grad_prob_flat.reshape(MICRO, TOKENS, TOPK)
    grad_down = down_grads.reshape(N_EXP, EXPERTS // N_EXP * FF, D)
    return grad_tokens, grad_probs, grad_down
```

```python
import functools

import jax
import jax.numpy as jnp
from jax import lax
from jax.experimental import pallas as pl
from jax.experimental.pallas import tpu as pltpu
from jax.sharding import PartitionSpec as P

MESH = pl.DeviceIdType.MESH
FF = 1536
TOPK = 8
EXPERTS = 128
MICRO = 2
CAP = 8
N_EXP = 16
N_Z = 12
N_Y = 4
PER_GROUP = EXPERTS // N_EXP
TOK = 64
D = 2048
UNITS = 256
WIDE = D + 128
HALF = 1152
CHUNK_ROWS = 32
CHUNK_COLS = 384
BF16 = jnp.bfloat16
F32 = jnp.float32


def flip(a, d):
    out = 0
    for bit in (1, 2, 4, 8):
        out = out + ((a // bit + d // bit) % 2) * bit
    return out


def kernel(
    tok_ref, cot_ref, ids_ref, probs_ref, gate_hbm, up_hbm, down_hbm,
    gtok_ref, gprob_ref, gdown_ref,
    weights, pick, send_f, recv_f, send_r, recv_r, red, recv_z, part_y, fin, gdown, wact_buf,
    w_sem, out_sem, sf_sem, rf_sem, sr_sem, rr_sem, sz_sem, rz_sem, sy_sem, ry_sem, sg_sem, rg_sem,
):
    rep = lax.axis_index("rep")
    me = lax.axis_index("exp")
    z = rep // N_Y
    y_hi = rep % N_Y
    y_lo = me // 8

    def local_expert(r):
        return r * UNITS // FF

    def rep_of(m, d):
        if m == 0:
            return rep
        step = (d // 8) * (2 * y_lo - 1)
        return z * N_Y + (y_hi + step + N_Y) % N_Y

    def exp_peer(m, p):
        d = p + 1
        return (rep_of(m, d), flip(me, d))

    def z_peer(q):
        return (((z + q + 1) % N_Z) * N_Y + y_hi, me)

    def y_peer(q):
        return (z * N_Y + (y_hi + q + 1) % N_Y, me)

    weight_copies = [
        pltpu.make_async_copy(src, weights.at[pl.ds(UNITS * i, UNITS)], w_sem.at[i])
        for i, src in enumerate((gate_hbm, up_hbm, down_hbm))
    ]
    for copy in weight_copies:
        copy.start()

    barrier = pltpu.get_barrier_semaphore()

    def greet(device):
        pl.semaphore_signal(barrier, inc=1, device_id=device, device_id_type=MESH)

    @pl.loop(0, N_EXP - 1)
    def _(p):
        greet(exp_peer(0, p))

    @pl.loop(0, 8)
    def _(p):
        greet(exp_peer(1, p + 7))

    @pl.loop(0, N_Z - 1)
    def _(q):
        greet(z_peer(q))

    @pl.loop(0, N_Y - 1)
    def _(q):
        greet(y_peer(q))

    greeted = (N_EXP - 1) + 8 + (N_Z - 1) + (N_Y - 1)

    lane = lax.broadcasted_iota(jnp.int32, (1, 256), 1)
    lane_d = (lane // 16 + 1) % 16
    lane_half = (lane // 8) % 2
    lane_slot = (lane % 8).astype(F32)
    lane_exp = flip(me, lane_d)
    expert_lane = lax.broadcasted_iota(jnp.int32, (1, EXPERTS), 1)
    tri = (
        lax.broadcasted_iota(jnp.int32, (TOK, TOK), 0)
        > lax.broadcasted_iota(jnp.int32, (TOK, TOK), 1)
    ).astype(BF16)

    def prepare(m):
        ids = ids_ref[m]
        probs = probs_ref[m].astype(F32)
        if m == 0:
            group = local_expert(rep)
        else:
            near, far = local_expert(rep), local_expert(rep_of(1, 8))
            group = near + (lane_d // 8) * (far - near)
        lane_expert = lane_exp * PER_GROUP + group
        member = jnp.zeros((TOK, 256), F32)
        table = jnp.zeros((TOK, EXPERTS), F32)
        for k in range(TOPK):
            column = ids[:, k : k + 1]
            member = member + jnp.where(column == lane_expert, 1.0, 0.0)
            table = table + jnp.where(column == expert_lane, probs[:, k : k + 1], 0.0)
        before = jnp.dot(tri, member.astype(BF16), preferred_element_type=F32)
        one_hot = jnp.where(before == lane_slot, member, 0.0)
        first = jnp.where(lane_half == 0, one_hot, 0.0)
        second = jnp.where(lane_half == 1, one_hot, 0.0)
        pick[m] = jnp.concatenate([first, second], axis=0).astype(BF16)
        rows = jnp.concatenate([tok_ref[m], cot_ref[m]], axis=0)
        table = table.astype(BF16)
        tables = jnp.concatenate([table, table], axis=0)
        chosen = pick[m]
        for start, size, source in ((0, 1024, rows[:, :1024]), (1024, 1024, rows[:, 1024:]), (D, 128, tables)):
            out = lax.dot_general(
                chosen, source, (((0,), (0,)), ((), ())), preferred_element_type=F32
            ).astype(BF16).reshape(16, 16, size)
            send_f[m, :, :, start : start + size] = out[:15]
            recv_f[m, 15, :, start : start + size] = out[15]

    def start_all(count, src, dst, send_sem, recv_sem, peer):
        @pl.loop(0, count)
        def _(i):
            pltpu.make_async_remote_copy(
                src_ref=src(i), dst_ref=dst(i), send_sem=send_sem, recv_sem=recv_sem,
                device_id=peer(i), device_id_type=MESH,
            ).start()

    def wait_for(ref, sem):
        pltpu.make_async_copy(ref, ref, sem).wait()

    def send_forward(m):
        start_all(
            15, lambda p: send_f.at[m, p], lambda p: recv_f.at[m, p],
            sf_sem.at[m], rf_sem.at[m], functools.partial(exp_peer, m),
        )

    def compute(m):
        rows = recv_f[m].reshape(256, WIDE)
        pre = lax.dot_general(
            rows[:, :D], weights[...], (((1,), (1,)), ((), ())), preferred_element_type=F32
        ).reshape(16, 2, 8, 3 * UNITS)
        gate_pre = pre[:, 0, :, :UNITS].reshape(128, UNITS)
        up_pre = pre[:, 0, :, UNITS : 2 * UNITS].reshape(128, UNITS)
        act_grad = pre[:, 1, :, 2 * UNITS :].reshape(128, UNITS)
        mine = (expert_lane == me * PER_GROUP + local_expert(rep)).astype(F32)
        prob = rows[:, D:].astype(F32).reshape(16, 2, 8, 128)[:, 0].reshape(128, 128)
        prob = jnp.sum(prob * mine, axis=1, keepdims=True)
        sigmoid_gate = jax.nn.sigmoid(gate_pre)
        silu_gate = gate_pre * sigmoid_gate
        act = silu_gate * up_pre
        prob_part = jnp.sum(act * act_grad, axis=1, keepdims=True)
        wact = (prob * act).reshape(16, 1, 8, UNITS)
        scaled = prob * act_grad
        gate_grad = scaled * up_pre * sigmoid_gate * (1.0 + gate_pre * (1.0 - sigmoid_gate))
        up_grad = scaled * silu_gate
        wact_buf[m] = (
            jnp.concatenate([jnp.zeros_like(wact), wact], axis=1).reshape(256, UNITS).astype(BF16)
        )
        grads = jnp.concatenate([gate_grad, up_grad], axis=1).astype(BF16)
        left = jnp.dot(grads, weights[: 2 * UNITS, :HALF], preferred_element_type=F32)
        right = jnp.dot(grads, weights[: 2 * UNITS, HALF:], preferred_element_type=F32)
        right = jnp.concatenate([right, prob_part * mine, jnp.zeros((128, 128), F32)], axis=1)
        out = jnp.concatenate(
            [left.reshape(16, 8, HALF), right.reshape(16, 8, HALF)], axis=1
        ).astype(BF16)
        send_r[m] = out[:15]
        recv_r[m, 15] = out[15]

    def send_back(m):
        start_all(
            15, lambda p: send_r.at[m, p], lambda p: recv_r.at[m, p],
            sr_sem.at[m], rr_sem.at[m], functools.partial(exp_peer, m),
        )

    def combine(m):
        total = jnp.dot(
            pick[m], recv_r[m].reshape(256, HALF), preferred_element_type=F32
        ).astype(BF16)
        for c in range(N_Z):
            i, j = c // 3, c % 3
            red[m, c] = total[
                CHUNK_ROWS * i : CHUNK_ROWS * (i + 1), CHUNK_COLS * j : CHUNK_COLS * (j + 1)
            ]

    def send_z(m):
        start_all(
            N_Z - 1, lambda q: red.at[m, (z + q + 1) % N_Z], lambda q: recv_z.at[m, q],
            sz_sem.at[m], rz_sem.at[m], z_peer,
        )

    def sum_z(m):
        total = red[m, z].astype(F32)
        for q in range(N_Z - 1):
            total = total + recv_z[m, q].astype(F32)
        part_y[m, y_hi] = total.astype(BF16)

    def send_y(m):
        start_all(
            N_Y - 1, lambda q: part_y.at[m, y_hi], lambda q: part_y.at[m, y_hi],
            sy_sem.at[m], ry_sem.at[m], y_peer,
        )

    def sum_y(m):
        total = part_y[m, 0].astype(F32)
        for q in range(1, N_Y):
            total = total + part_y[m, q].astype(F32)
        fin[m, z] = total.astype(BF16)

    def send_out(m):
        start_all(
            N_Z - 1, lambda q: fin.at[m, z], lambda q: fin.at[m, z],
            sg_sem.at[m], rg_sem.at[m], z_peer,
        )

    def finish(m):
        for c in range(N_Z):
            i, j = c // 3, c % 3
            row = CHUNK_ROWS * (i % 2)
            col = HALF * (i // 2) + CHUNK_COLS * j
            size = min(CHUNK_COLS, D - col)
            gtok_ref[m, row : row + CHUNK_ROWS, col : col + size] = fin[m, c, :, :size]
        ids = ids_ref[m]
        table = jnp.concatenate(
            [fin[m, 8, :, 128:256], fin[m, 11, :, 128:256]], axis=0
        ).astype(F32)
        columns = [
            jnp.sum(jnp.where(ids[:, k : k + 1] == expert_lane, table, 0.0), axis=1, keepdims=True)
            for k in range(TOPK)
        ]
        gprob_ref[m] = jnp.concatenate(columns, axis=1)

    prepare(0)
    pl.semaphore_wait(barrier, greeted)
    send_forward(0)
    prepare(1)
    send_forward(1)
    for copy in weight_copies:
        copy.wait()

    wait_for(recv_f.at[0, pl.ds(0, 15)], rf_sem.at[0])
    compute(0)
    send_back(0)
    wait_for(recv_f.at[1, pl.ds(0, 15)], rf_sem.at[1])
    compute(1)
    send_back(1)

    acts = wact_buf[...].reshape(512, UNITS)
    for part in range(4):
        cols = slice(512 * part, 512 * (part + 1))
        gdown[:, cols] = lax.dot_general(
            acts, recv_f[:, :, :, cols].reshape(512, 512), (((0,), (0,)), ((), ())),
            preferred_element_type=F32,
        ).astype(BF16)
    out_copy = pltpu.make_async_copy(gdown, gdown_ref, out_sem)
    out_copy.start()

    wait_for(recv_r.at[0, pl.ds(0, 15)], rr_sem.at[0])
    combine(0)
    send_z(0)
    wait_for(recv_r.at[1, pl.ds(0, 15)], rr_sem.at[1])
    combine(1)
    send_z(1)
    for m in range(MICRO):
        wait_for(recv_z.at[m], rz_sem.at[m])
        sum_z(m)
        send_y(m)
        wait_for(part_y.at[m, pl.ds(0, N_Y - 1)], ry_sem.at[m])
        sum_y(m)
        send_out(m)
    for m in range(MICRO):
        wait_for(fin.at[m, pl.ds(0, N_Z - 1)], rg_sem.at[m])
        finish(m)
    out_copy.wait()
    for m in range(MICRO):
        wait_for(send_f.at[m], sf_sem.at[m])
        wait_for(send_r.at[m], sr_sem.at[m])
        wait_for(recv_z.at[m], sz_sem.at[m])
        wait_for(part_y.at[m, pl.ds(0, N_Y - 1)], sy_sem.at[m])
        wait_for(fin.at[m, pl.ds(0, N_Z - 1)], sg_sem.at[m])


def body(tokens, cotangent, expert_ids, route_probs, gate_weight, up_weight, down_weight):
    vmem = pl.BlockSpec(memory_space=pltpu.VMEM)
    hbm = pl.BlockSpec(memory_space=pl.ANY)
    gtok, gprob, gdown = pl.pallas_call(
        kernel,
        name="expert_backward",
        out_shape=(
            jax.ShapeDtypeStruct((MICRO, TOK, D), BF16),
            jax.ShapeDtypeStruct((MICRO, TOK, TOPK), F32),
            jax.ShapeDtypeStruct((UNITS, D), BF16),
        ),
        in_specs=[vmem] * 4 + [hbm] * 3,
        out_specs=(vmem, vmem, hbm),
        scratch_shapes=[
            pltpu.VMEM((3 * UNITS, D), BF16),
            pltpu.VMEM((MICRO, 128, 256), BF16),
            pltpu.VMEM((MICRO, 15, 16, WIDE), BF16),
            pltpu.VMEM((MICRO, 16, 16, WIDE), BF16),
            pltpu.VMEM((MICRO, 15, 16, HALF), BF16),
            pltpu.VMEM((MICRO, 16, 16, HALF), BF16),
            pltpu.VMEM((MICRO, N_Z, CHUNK_ROWS, CHUNK_COLS), BF16),
            pltpu.VMEM((MICRO, N_Z - 1, CHUNK_ROWS, CHUNK_COLS), BF16),
            pltpu.VMEM((MICRO, N_Y, CHUNK_ROWS, CHUNK_COLS), BF16),
            pltpu.VMEM((MICRO, N_Z, CHUNK_ROWS, CHUNK_COLS), BF16),
            pltpu.VMEM((UNITS, D), BF16),
            pltpu.VMEM((MICRO, 256, UNITS), BF16),
            pltpu.SemaphoreType.DMA((3,)),
            pltpu.SemaphoreType.DMA,
        ] + [pltpu.SemaphoreType.DMA((MICRO,))] * 10,
        compiler_params=pltpu.CompilerParams(
            collective_id=0, has_side_effects=True, vmem_limit_bytes=48 << 20
        ),
    )(
        tokens, cotangent, expert_ids, route_probs,
        gate_weight[0], up_weight[0], down_weight[0],
    )
    return gtok, gprob, gdown[None]


def solution(mesh):
    return jax.shard_map(
        body,
        mesh=mesh,
        in_specs=(
            P(None, "exp", None),
            P(None, "exp", None),
            P(None, "exp", None),
            P(None, "exp", None),
            P("exp", "rep", None),
            P("exp", "rep", None),
            P("exp", "rep", None),
        ),
        out_specs=(P(None, "exp", None), P(None, "exp", None), P("exp", "rep", None)),
        check_vma=False,
    )
```

```python
import jax
import jax.numpy as jnp
from jax import lax
from jax.experimental import pallas as pl
from jax.experimental.pallas import tpu as pltpu
from jax.sharding import PartitionSpec as P

MESH = pl.DeviceIdType.MESH
FF = 1536
TOPK = 8
EXPERTS = 128
MICRO = 2
CAP = 8
N_EXP = 16
N_Z = 12
N_Y = 4
N_K = 4
N_J = N_Z // N_K
PER_GROUP = EXPERTS // N_EXP
TOK = 64
D = 2048
UNITS = 256
WIDE = D + 128
HALF = 1152
CHUNK_ROWS = 32
CHUNK_COLS = 384
BF16 = jnp.bfloat16
F32 = jnp.float32


def flip(a, d):
    out = 0
    for bit in (1, 2, 4, 8):
        out = out + ((a // bit + d // bit) % 2) * bit
    return out


def kernel(
    tok_hbm, cot_hbm, ids_hbm, probs_hbm, gate_hbm, up_hbm, down_hbm,
    gtok_ref, gprob_ref, gdown_ref,
    rows_ref, ids_ref, probs_ref, weights, pick, send_f, recv_f, send_r, recv_r,
    red, recv_s, part_z, recv_w, part_y, fin, gdown, wact_buf,
    in_sem, w_sem, out_sem,
    sf_sem, rf_sem, sr_sem, rr_sem, s1_sem, r1_sem, s2_sem, r2_sem,
    sy_sem, ry_sem, s3_sem, r3_sem, s4_sem, r4_sem,
):
    rep = lax.axis_index("rep")
    me = lax.axis_index("exp")
    z = rep // N_Y
    y_hi = rep % N_Y
    y_lo = me // 8
    core = me % 2
    kind = z % N_K
    turn = z // N_K

    def local_expert(r):
        return r * UNITS // FF

    def rep_of(m, d):
        if m == 0:
            return rep
        step = (d // 8) * (2 * y_lo - 1)
        return z * N_Y + (y_hi + step + N_Y) % N_Y

    def exp_peer(m, p):
        d = p + 1
        return (rep_of(m, d), flip(me, d))

    def z_peer(step):
        return (((z + step + N_Z) % N_Z) * N_Y + y_hi, me)

    def y_peer(q):
        return (z * N_Y + (y_hi + q + 1) % N_Y, me)

    input_copies = [
        pltpu.make_async_copy(src, dst, in_sem.at[i])
        for i, (src, dst) in enumerate((
            (ids_hbm, ids_ref),
            (probs_hbm, probs_ref),
            (tok_hbm.at[0], rows_ref.at[0, pl.ds(0, TOK)]),
            (cot_hbm.at[0], rows_ref.at[0, pl.ds(TOK, TOK)]),
            (tok_hbm.at[1], rows_ref.at[1, pl.ds(0, TOK)]),
            (cot_hbm.at[1], rows_ref.at[1, pl.ds(TOK, TOK)]),
        ))
    ]
    weight_copies = [
        pltpu.make_async_copy(src, weights.at[pl.ds(UNITS * i, UNITS)], w_sem.at[i])
        for i, src in enumerate((gate_hbm, up_hbm, down_hbm))
    ]
    for copy in input_copies:
        copy.start()
    for copy in weight_copies:
        copy.start()

    barrier = pltpu.get_barrier_semaphore()

    def greet(device):
        pl.semaphore_signal(barrier, inc=1, device_id=device, device_id_type=MESH)

    @pl.loop(0, N_EXP - 1)
    def _(p):
        greet(exp_peer(0, p))

    @pl.loop(0, 8)
    def _(p):
        greet(exp_peer(1, p + 7))

    for step in (1, -1, 2, -2, 4, -4):
        greet(z_peer(step))

    @pl.loop(0, N_Y - 1)
    def _(q):
        greet(y_peer(q))

    greeted = (N_EXP - 1) + 8 + 6 + (N_Y - 1)

    row = lax.broadcasted_iota(jnp.int32, (256, 1), 0)
    row_d = (row // 16 + 1) % 16
    row_half = (row // 8) % 2
    row_slot = (row % 8).astype(F32)
    row_exp = flip(me, row_d)
    expert_lane = lax.broadcasted_iota(jnp.int32, (1, EXPERTS), 1)
    expert_row = lax.broadcasted_iota(jnp.int32, (EXPERTS, 1), 0)
    earlier = (
        lax.broadcasted_iota(jnp.int32, (TOK, TOK), 0)
        < lax.broadcasted_iota(jnp.int32, (TOK, TOK), 1)
    ).astype(BF16)

    def prepare(m):
        ids = ids_ref[m]
        probs = probs_ref[m].astype(F32)
        if m == 0:
            group = local_expert(rep)
        else:
            near, far = local_expert(rep), local_expert(rep_of(1, 8))
            group = near + (row_d // 8) * (far - near)
        row_expert = row_exp * PER_GROUP + group
        member = jnp.zeros((256, TOK), F32)
        table = jnp.zeros((EXPERTS, TOK), F32)
        for k in range(TOPK):
            route = ids[k : k + 1]
            member = member + jnp.where(route == row_expert, 1.0, 0.0)
            table = table + jnp.where(route == expert_row, probs[k : k + 1], 0.0)
        before = jnp.dot(member.astype(BF16), earlier, preferred_element_type=F32)
        one_hot = jnp.where(before == row_slot, member, 0.0)
        first = jnp.where(row_half == 0, one_hot, 0.0)
        second = jnp.where(row_half == 1, one_hot, 0.0)
        chosen = jnp.concatenate([first, second], axis=1).astype(BF16)
        pick[m] = chosen

        def put(start, size, out):
            out = out.astype(BF16).reshape(16, 16, size)
            send_f[m, :, :, start : start + size] = out[:15]
            recv_f[m, 15, :, start : start + size] = out[15]

        for start in (0, 1024):
            put(start, 1024, jnp.dot(
                chosen, rows_ref[m, :, start : start + 1024], preferred_element_type=F32
            ))
        put(D, 128, lax.dot_general(
            one_hot.astype(BF16), table.astype(BF16), (((1,), (1,)), ((), ())),
            preferred_element_type=F32,
        ))

    def start_all(count, src, dst, send_sem, recv_sem, peer):
        @pl.loop(0, count)
        def _(i):
            pltpu.make_async_remote_copy(
                src_ref=src(i), dst_ref=dst(i), send_sem=send_sem, recv_sem=recv_sem,
                device_id=peer(i), device_id_type=MESH,
            ).start()

    def wait_for(ref, sem):
        pltpu.make_async_copy(ref, ref, sem).wait()

    def place(i):
        return ((5 + 6 * core) * (i + 1)) % N_EXP - 1

    def send_forward(m):
        start_all(
            15, lambda i: send_f.at[m, place(i)], lambda i: recv_f.at[m, place(i)],
            sf_sem.at[m], rf_sem.at[m], lambda i: exp_peer(m, place(i)),
        )

    def compute(m):
        rows = recv_f[m].reshape(256, WIDE)
        pre = lax.dot_general(
            rows[:, :D], weights[...], (((1,), (1,)), ((), ())), preferred_element_type=F32
        ).reshape(16, 2, 8, 3 * UNITS)
        gate_pre = pre[:, 0, :, :UNITS].reshape(128, UNITS)
        up_pre = pre[:, 0, :, UNITS : 2 * UNITS].reshape(128, UNITS)
        act_grad = pre[:, 1, :, 2 * UNITS :].reshape(128, UNITS)
        mine = (expert_lane == me * PER_GROUP + local_expert(rep)).astype(F32)
        prob = rows[:, D:].astype(F32).reshape(16, 2, 8, 128)[:, 0].reshape(128, 128)
        prob = jnp.sum(prob * mine, axis=1, keepdims=True)
        sigmoid_gate = jax.nn.sigmoid(gate_pre)
        silu_gate = gate_pre * sigmoid_gate
        act = silu_gate * up_pre
        prob_part = jnp.sum(act * act_grad, axis=1, keepdims=True)
        wact = (prob * act).reshape(16, 1, 8, UNITS)
        scaled = prob * act_grad
        gate_grad = scaled * up_pre * sigmoid_gate * (1.0 + gate_pre * (1.0 - sigmoid_gate))
        up_grad = scaled * silu_gate
        wact_buf[m] = (
            jnp.concatenate([jnp.zeros_like(wact), wact], axis=1).reshape(256, UNITS).astype(BF16)
        )
        grads = jnp.concatenate([gate_grad, up_grad], axis=1).astype(BF16)
        left = jnp.dot(grads, weights[: 2 * UNITS, :HALF], preferred_element_type=F32)
        right = jnp.dot(grads, weights[: 2 * UNITS, HALF:], preferred_element_type=F32)
        right = jnp.concatenate([right, prob_part * mine, jnp.zeros((128, 128), F32)], axis=1)
        out = jnp.concatenate(
            [left.reshape(16, 8, HALF), right.reshape(16, 8, HALF)], axis=1
        ).astype(BF16)
        send_r[m] = out[:15]
        recv_r[m, 15] = out[15]

    def send_back(m):
        start_all(
            15, lambda i: send_r.at[m, place(i)], lambda i: recv_r.at[m, place(i)],
            sr_sem.at[m], rr_sem.at[m], lambda i: exp_peer(m, place(i)),
        )

    def combine(m):
        total = lax.dot_general(
            pick[m], recv_r[m].reshape(256, HALF), (((0,), (0,)), ((), ())),
            preferred_element_type=F32,
        ).astype(BF16)
        for c in range(N_Z):
            i, j = c // 3, c % 3
            red[m, i, j] = total[
                CHUNK_ROWS * i : CHUNK_ROWS * (i + 1), CHUNK_COLS * j : CHUNK_COLS * (j + 1)
            ]

    def start_one(src, dst, send_sem, recv_sem, device):
        pltpu.make_async_remote_copy(
            src_ref=src, dst_ref=dst, send_sem=send_sem, recv_sem=recv_sem,
            device_id=device, device_id_type=MESH,
        ).start()

    low, high = pl.ds(0, CHUNK_ROWS // 2), pl.ds(CHUNK_ROWS // 2, CHUNK_ROWS // 2)

    def send_near(m):
        across = (kind + 2) % N_K
        for step, rows in ((2, low), (-2, high)):
            start_one(
                red.at[m, across, :, rows], recv_s.at[m, 2, :, rows],
                s1_sem.at[m], r1_sem.at[m], z_peer(step),
            )
        for slot, step in enumerate((1, -1)):
            start_one(
                red.at[m, (kind + step + N_K) % N_K], recv_s.at[m, slot],
                s1_sem.at[m], r1_sem.at[m], z_peer(step),
            )

    def sum_near(m):
        total = red[m, kind].astype(F32)
        for slot in range(3):
            total = total + recv_s[m, slot].astype(F32)
        part_z[m] = total.astype(BF16)

    def send_far(m):
        for slot, step in enumerate((1, 2)):
            start_one(
                part_z.at[m, (turn + step) % N_J], recv_w.at[m, slot],
                s2_sem.at[m], r2_sem.at[m], z_peer(step * N_K),
            )

    def sum_far(m):
        total = part_z[m, turn].astype(F32)
        for slot in range(N_J - 1):
            total = total + recv_w[m, slot].astype(F32)
        part_y[m, y_hi] = total.astype(BF16)

    def send_y(m):
        start_all(
            N_Y - 1, lambda q: part_y.at[m, y_hi], lambda q: part_y.at[m, y_hi],
            sy_sem.at[m], ry_sem.at[m], y_peer,
        )

    def sum_y(m):
        total = part_y[m, 0].astype(F32)
        for q in range(1, N_Y):
            total = total + part_y[m, q].astype(F32)
        fin[m, kind, turn] = total.astype(BF16)

    def give_far(m):
        for step in (1, 2):
            start_one(
                fin.at[m, kind, turn], fin.at[m, kind, turn],
                s3_sem.at[m], r3_sem.at[m], z_peer(step * N_K),
            )

    def give_near(m):
        for step, rows in ((2, low), (-2, high)):
            start_one(
                fin.at[m, kind, :, rows], fin.at[m, kind, :, rows],
                s4_sem.at[m], r4_sem.at[m], z_peer(step),
            )
        for step in (1, -1):
            start_one(
                fin.at[m, kind], fin.at[m, kind], s4_sem.at[m], r4_sem.at[m], z_peer(step)
            )

    def finish(m):
        for c in range(N_Z):
            i, j = c // 3, c % 3
            top = CHUNK_ROWS * (i % 2)
            col = HALF * (i // 2) + CHUNK_COLS * j
            size = min(CHUNK_COLS, D - col)
            gtok_ref[m, top : top + CHUNK_ROWS, col : col + size] = fin[m, i, j, :, :size]
        ids = ids_ref[m]
        table = jnp.concatenate(
            [fin[m, 2, 2, :, 128:256], fin[m, 3, 2, :, 128:256]], axis=0
        ).astype(F32).T
        gprob_ref[m] = jnp.concatenate(
            [
                jnp.sum(jnp.where(ids[k : k + 1] == expert_row, table, 0.0), axis=0, keepdims=True)
                for k in range(TOPK)
            ],
            axis=0,
        )

    def await_near(m):
        wait_for(recv_s.at[m], r1_sem.at[m])

    def await_far(m):
        wait_for(recv_w.at[m], r2_sem.at[m])

    def await_y(m):
        wait_for(part_y.at[m, pl.ds(0, N_Y - 1)], ry_sem.at[m])

    def await_given_far(m):
        wait_for(recv_w.at[m], r3_sem.at[m])

    def await_given_near(m):
        wait_for(recv_s.at[m], r4_sem.at[m])

    for copy in input_copies[:4]:
        copy.wait()
    prepare(0)
    pl.semaphore_wait(barrier, greeted)
    send_forward(0)
    for copy in input_copies[4:]:
        copy.wait()
    prepare(1)
    send_forward(1)
    for copy in weight_copies:
        copy.wait()

    wait_for(send_f.at[0], rf_sem.at[0])
    compute(0)
    send_back(0)
    wait_for(send_f.at[1], rf_sem.at[1])
    compute(1)
    send_back(1)
    wait_for(send_r.at[0], rr_sem.at[0])
    combine(0)
    send_near(0)

    acts = wact_buf[...].reshape(512, UNITS)
    for part in range(4):
        cols = slice(512 * part, 512 * (part + 1))
        gdown[:, cols] = lax.dot_general(
            acts, recv_f[:, :, :, cols].reshape(512, 512), (((0,), (0,)), ((), ())),
            preferred_element_type=F32,
        ).astype(BF16)
    out_copy = pltpu.make_async_copy(gdown, gdown_ref, out_sem)
    out_copy.start()

    await_near(0)
    sum_near(0)
    send_far(0)
    await_far(0)
    sum_far(0)
    send_y(0)
    wait_for(send_r.at[1], rr_sem.at[1])
    combine(1)
    send_near(1)
    await_y(0)
    sum_y(0)
    give_far(0)
    await_near(1)
    sum_near(1)
    send_far(1)
    await_given_far(0)
    give_near(0)
    await_far(1)
    sum_far(1)
    send_y(1)
    await_given_near(0)
    finish(0)
    await_y(1)
    sum_y(1)
    give_far(1)
    await_given_far(1)
    give_near(1)
    await_given_near(1)
    finish(1)
    out_copy.wait()
    for m in range(MICRO):
        wait_for(send_f.at[m], sf_sem.at[m])
        wait_for(send_r.at[m], sr_sem.at[m])
        wait_for(recv_s.at[m], s1_sem.at[m])
        wait_for(recv_w.at[m], s2_sem.at[m])
        wait_for(part_y.at[m, pl.ds(0, N_Y - 1)], sy_sem.at[m])
        wait_for(recv_w.at[m], s3_sem.at[m])
        wait_for(recv_s.at[m], s4_sem.at[m])


def body(tokens, cotangent, expert_ids, route_probs, gate_weight, up_weight, down_weight):
    vmem = pl.BlockSpec(memory_space=pltpu.VMEM)
    hbm = pl.BlockSpec(memory_space=pltpu.HBM)
    gtok, gprob, gdown = pl.pallas_call(
        kernel,
        name="expert_backward",
        out_shape=(
            jax.ShapeDtypeStruct((MICRO, TOK, D), BF16),
            jax.ShapeDtypeStruct((MICRO, TOPK, TOK), F32),
            jax.ShapeDtypeStruct((UNITS, D), BF16),
        ),
        in_specs=[hbm] * 7,
        out_specs=(vmem, vmem, pl.BlockSpec(memory_space=pl.ANY)),
        scratch_shapes=[
            pltpu.VMEM((MICRO, 2 * TOK, D), BF16),
            pltpu.VMEM((MICRO, TOPK, TOK), jnp.int32),
            pltpu.VMEM((MICRO, TOPK, TOK), BF16),
            pltpu.VMEM((3 * UNITS, D), BF16),
            pltpu.VMEM((MICRO, 256, 128), BF16),
            pltpu.VMEM((MICRO, 15, 16, WIDE), BF16),
            pltpu.VMEM((MICRO, 16, 16, WIDE), BF16),
            pltpu.VMEM((MICRO, 15, 16, HALF), BF16),
            pltpu.VMEM((MICRO, 16, 16, HALF), BF16),
            pltpu.VMEM((MICRO, N_K, N_J, CHUNK_ROWS, CHUNK_COLS), BF16),
            pltpu.VMEM((MICRO, 3, N_J, CHUNK_ROWS, CHUNK_COLS), BF16),
            pltpu.VMEM((MICRO, N_J, CHUNK_ROWS, CHUNK_COLS), BF16),
            pltpu.VMEM((MICRO, N_J - 1, CHUNK_ROWS, CHUNK_COLS), BF16),
            pltpu.VMEM((MICRO, N_Y, CHUNK_ROWS, CHUNK_COLS), BF16),
            pltpu.VMEM((MICRO, N_K, N_J, CHUNK_ROWS, CHUNK_COLS), BF16),
            pltpu.VMEM((UNITS, D), BF16),
            pltpu.VMEM((MICRO, 256, UNITS), BF16),
            pltpu.SemaphoreType.DMA((6,)),
            pltpu.SemaphoreType.DMA((3,)),
            pltpu.SemaphoreType.DMA,
        ] + [pltpu.SemaphoreType.DMA((MICRO,))] * 14,
        compiler_params=pltpu.CompilerParams(
            collective_id=0, has_side_effects=True, vmem_limit_bytes=60 << 20
        ),
    )(
        tokens, cotangent,
        jnp.transpose(expert_ids, (0, 2, 1)), jnp.transpose(route_probs, (0, 2, 1)),
        gate_weight[0], up_weight[0], down_weight[0],
    )
    return gtok, jnp.transpose(gprob, (0, 2, 1)), gdown[None]


def solution(mesh):
    return jax.shard_map(
        body,
        mesh=mesh,
        in_specs=(
            P(None, "exp", None),
            P(None, "exp", None),
            P(None, "exp", None),
            P(None, "exp", None),
            P("exp", "rep", None),
            P("exp", "rep", None),
            P("exp", "rep", None),
        ),
        out_specs=(P(None, "exp", None), P(None, "exp", None), P("exp", "rep", None)),
        check_vma=False,
    )
```

```python
import jax
import jax.numpy as jnp
from jax import lax
from jax.experimental import pallas as pl
from jax.experimental.pallas import tpu as pltpu
from jax.sharding import PartitionSpec as P

MESH = pl.DeviceIdType.MESH
FF = 1536
TOPK = 8
EXPERTS = 128
MICRO = 2
CAP = 8
N_EXP = 16
N_Z = 12
N_Y = 4
N_K = 4
N_T = N_Z // N_K
N_C = 9
N_OWN = N_C // N_T
PER_GROUP = EXPERTS // N_EXP
TOK = 64
D = 2048
UNITS = 256
WIDE = D + 128
HALF = 1152
CHUNK = (32, 128)
BF16 = jnp.bfloat16
F32 = jnp.float32


def flip(a, d):
    out = 0
    for bit in (1, 2, 4, 8):
        out = out + ((a // bit + d // bit) % 2) * bit
    return out


def kernel(
    tok_hbm, cot_hbm, ids_hbm, probs_hbm, gate_hbm, up_hbm, down_hbm,
    gtok_ref, gprob_ref, gdown_ref,
    rows_ref, ids_ref, probs_ref, weights, pick, send_f, recv_f, send_r, recv_r,
    red, recv_s, part_z, recv_w, fin, gdown, wact_buf,
    in_sem, w_sem, out_sem,
    sf_sem, rf_sem, sr_sem, rr_sem, s1_sem, r1_sem, s2_sem, r2_sem,
    s3_sem, r3_sem, s4_sem, r4_sem,
):
    rep = lax.axis_index("rep")
    me = lax.axis_index("exp")
    z = rep // N_Y
    y_hi = rep % N_Y
    y_lo = me // 8
    core = me % 2
    kind = z % N_K
    turn = z // N_K

    def local_expert(r):
        return r * UNITS // FF

    def far_side(m, d):
        return (d // 8) * ((d + m) % 2)

    def rep_of(m, d):
        step = far_side(m, d) * (2 * y_lo - 1)
        return z * N_Y + (y_hi + step + N_Y) % N_Y

    def exp_peer(m, p):
        d = p + 1
        return (rep_of(m, d), flip(me, d))

    def z_peer(step):
        return (((z + step + N_Z) % N_Z) * N_Y + y_hi, me)

    def kin(q):
        to_turn, to_y = (turn + q // N_Y) % N_T, (y_hi + q) % N_Y
        return ((to_turn * N_K + kind) * N_Y + to_y, me), to_turn * N_OWN + to_y, to_y < N_OWN

    input_copies = [
        pltpu.make_async_copy(src, dst, in_sem.at[i])
        for i, (src, dst) in enumerate((
            (ids_hbm, ids_ref),
            (probs_hbm, probs_ref),
            (tok_hbm.at[0], rows_ref.at[0, pl.ds(0, TOK)]),
            (cot_hbm.at[0], rows_ref.at[0, pl.ds(TOK, TOK)]),
            (tok_hbm.at[1], rows_ref.at[1, pl.ds(0, TOK)]),
            (cot_hbm.at[1], rows_ref.at[1, pl.ds(TOK, TOK)]),
        ))
    ]
    weight_copies = [
        pltpu.make_async_copy(src, weights.at[pl.ds(UNITS * i, UNITS)], w_sem.at[i])
        for i, src in enumerate((gate_hbm, up_hbm, down_hbm))
    ]
    for copy in input_copies:
        copy.start()
    for copy in weight_copies:
        copy.start()

    barrier = pltpu.get_barrier_semaphore()

    def greet(device):
        pl.semaphore_signal(barrier, inc=1, device_id=device, device_id_type=MESH)

    @pl.loop(0, N_EXP - 1)
    def _(p):
        greet(exp_peer(0, p))

    @pl.loop(7, N_EXP - 1)
    def _(p):
        greet(exp_peer(1, p))

    for step in (1, -1, 2, -2):
        greet(z_peer(step))

    @pl.loop(1, N_T * N_Y)
    def _(q):
        greet(kin(q)[0])

    greeted = (N_EXP - 1) + 8 + 4 + (N_T * N_Y - 1)

    row = lax.broadcasted_iota(jnp.int32, (256, 1), 0)
    row_d = (row // 16 + 1) % 16
    row_half = (row // 8) % 2
    row_slot = (row % 8).astype(F32)
    row_exp = flip(me, row_d)
    expert_lane = lax.broadcasted_iota(jnp.int32, (1, EXPERTS), 1)
    expert_row = lax.broadcasted_iota(jnp.int32, (EXPERTS, 1), 0)
    earlier = (
        lax.broadcasted_iota(jnp.int32, (TOK, TOK), 0)
        < lax.broadcasted_iota(jnp.int32, (TOK, TOK), 1)
    ).astype(BF16)

    def prepare(m):
        ids = ids_ref[m]
        probs = probs_ref[m].astype(F32)
        near, far = local_expert(rep), local_expert(rep_of(m, 9 - m))
        group = near + far_side(m, row_d) * (far - near)
        row_expert = row_exp * PER_GROUP + group
        member = jnp.zeros((256, TOK), F32)
        table = jnp.zeros((EXPERTS, TOK), F32)
        for k in range(TOPK):
            route = ids[k : k + 1]
            member = member + jnp.where(route == row_expert, 1.0, 0.0)
            table = table + jnp.where(route == expert_row, probs[k : k + 1], 0.0)
        before = jnp.dot(member.astype(BF16), earlier, preferred_element_type=F32)
        one_hot = jnp.where(before == row_slot, member, 0.0)
        first = jnp.where(row_half == 0, one_hot, 0.0)
        second = jnp.where(row_half == 1, one_hot, 0.0)
        chosen = jnp.concatenate([first, second], axis=1).astype(BF16)
        pick[m] = chosen

        def put(start, size, out):
            out = out.astype(BF16).reshape(16, 16, size)
            send_f[m, :, :, start : start + size] = out[:15]
            recv_f[m, 15, :, start : start + size] = out[15]

        for start in (0, 1024):
            put(start, 1024, jnp.dot(
                chosen, rows_ref[m, :, start : start + 1024], preferred_element_type=F32
            ))
        put(D, 128, lax.dot_general(
            one_hot.astype(BF16), table.astype(BF16), (((1,), (1,)), ((), ())),
            preferred_element_type=F32,
        ))

    def start_all(count, src, dst, send_sem, recv_sem, peer):
        @pl.loop(0, count)
        def _(i):
            pltpu.make_async_remote_copy(
                src_ref=src(i), dst_ref=dst(i), send_sem=send_sem, recv_sem=recv_sem,
                device_id=peer(i), device_id_type=MESH,
            ).start()

    def wait_for(ref, sem):
        pltpu.make_async_copy(ref, ref, sem).wait()

    def place(i):
        return ((5 + 6 * core) * (i + 1)) % N_EXP - 1

    def send_forward(m):
        start_all(
            15, lambda i: send_f.at[m, place(i)], lambda i: recv_f.at[m, place(i)],
            sf_sem.at[m], rf_sem.at[m], lambda i: exp_peer(m, place(i)),
        )

    def compute(m):
        rows = recv_f[m].reshape(256, WIDE)
        pre = lax.dot_general(
            rows[:, :D], weights[...], (((1,), (1,)), ((), ())), preferred_element_type=F32
        ).reshape(16, 2, 8, 3 * UNITS)
        gate_pre = pre[:, 0, :, :UNITS].reshape(128, UNITS)
        up_pre = pre[:, 0, :, UNITS : 2 * UNITS].reshape(128, UNITS)
        act_grad = pre[:, 1, :, 2 * UNITS :].reshape(128, UNITS)
        mine = (expert_lane == me * PER_GROUP + local_expert(rep)).astype(F32)
        prob = rows[:, D:].astype(F32).reshape(16, 2, 8, 128)[:, 0].reshape(128, 128)
        prob = jnp.sum(prob * mine, axis=1, keepdims=True)
        sigmoid_gate = jax.nn.sigmoid(gate_pre)
        silu_gate = gate_pre * sigmoid_gate
        act = silu_gate * up_pre
        prob_part = jnp.sum(act * act_grad, axis=1, keepdims=True)
        wact = (prob * act).reshape(16, 1, 8, UNITS)
        scaled = prob * act_grad
        gate_grad = scaled * up_pre * sigmoid_gate * (1.0 + gate_pre * (1.0 - sigmoid_gate))
        up_grad = scaled * silu_gate
        wact_buf[m] = (
            jnp.concatenate([jnp.zeros_like(wact), wact], axis=1).reshape(256, UNITS).astype(BF16)
        )
        grads = jnp.concatenate([gate_grad, up_grad], axis=1).astype(BF16)
        left = jnp.dot(grads, weights[: 2 * UNITS, :HALF], preferred_element_type=F32)
        right = jnp.dot(grads, weights[: 2 * UNITS, HALF:], preferred_element_type=F32)
        right = jnp.concatenate([right, prob_part * mine, jnp.zeros((128, 128), F32)], axis=1)
        out = jnp.concatenate(
            [left.reshape(16, 8, HALF), right.reshape(16, 8, HALF)], axis=1
        ).astype(BF16)
        send_r[m] = out[:15]
        recv_r[m, 15] = out[15]

    def send_back(m):
        start_all(
            15, lambda i: send_r.at[m, place(i)], lambda i: recv_r.at[m, place(i)],
            sr_sem.at[m], rr_sem.at[m], lambda i: exp_peer(m, place(i)),
        )

    def combine(m):
        total = lax.dot_general(
            pick[m], recv_r[m].reshape(256, HALF), (((0,), (0,)), ((), ())),
            preferred_element_type=F32,
        ).astype(BF16)
        for k in range(N_K):
            for c in range(N_C):
                red[m, k, c] = total[32 * k : 32 * (k + 1), 128 * c : 128 * (c + 1)]

    def start_one(src, dst, send_sem, recv_sem, device):
        pltpu.make_async_remote_copy(
            src_ref=src, dst_ref=dst, send_sem=send_sem, recv_sem=recv_sem,
            device_id=device, device_id_type=MESH,
        ).start()

    low, high = pl.ds(0, 5), pl.ds(5, N_C - 5)
    owner = y_hi < N_OWN
    own = turn * N_OWN + y_hi

    def send_near(m):
        across = (kind + 2) % N_K
        for step, part in ((2, low), (-2, high)):
            start_one(
                red.at[m, across, part], recv_s.at[m, 2, part],
                s1_sem.at[m], r1_sem.at[m], z_peer(step),
            )
        for slot, step in enumerate((1, -1)):
            start_one(
                red.at[m, (kind + step + N_K) % N_K], recv_s.at[m, slot],
                s1_sem.at[m], r1_sem.at[m], z_peer(step),
            )

    def await_near(m):
        wait_for(recv_s.at[m], r1_sem.at[m])
        total = red[m, kind].astype(F32)
        for slot in range(3):
            total = total + recv_s[m, slot].astype(F32)
        part_z[m] = total.astype(BF16)

    def send_kin(m):
        @pl.loop(1, N_T * N_Y)
        def _(q):
            device, chunk, owns = kin(q)

            @pl.when(owns)
            def _():
                start_one(
                    part_z.at[m, chunk], recv_w.at[m, q - 1], s2_sem.at[m], r2_sem.at[m], device
                )

    def await_kin(m):
        @pl.when(owner)
        def _():
            wait_for(recv_w.at[m], r2_sem.at[m])
            total = part_z[m, own].astype(F32)
            for slot in range(N_T * N_Y - 1):
                total = total + recv_w[m, slot].astype(F32)
            fin[m, kind, own] = total.astype(BF16)

    def give_kin(m):
        @pl.when(owner)
        def _():
            @pl.loop(1, N_T * N_Y)
            def _(q):
                start_one(
                    fin.at[m, kind, own], fin.at[m, kind, own],
                    s3_sem.at[m], r3_sem.at[m], kin(q)[0],
                )

    def wait_but_own(ref, sem):
        @pl.when(owner)
        def _():
            wait_for(ref.at[pl.ds(0, N_C - 1)], sem)

        @pl.when(jnp.logical_not(owner))
        def _():
            wait_for(ref.at[pl.ds(0, N_C)], sem)

    def await_given_kin(m):
        wait_but_own(recv_w.at[m], r3_sem.at[m])

    def give_near(m):
        for step, part in ((2, low), (-2, high)):
            start_one(
                fin.at[m, kind, part], fin.at[m, kind, part],
                s4_sem.at[m], r4_sem.at[m], z_peer(step),
            )
        for step in (1, -1):
            start_one(
                fin.at[m, kind], fin.at[m, kind], s4_sem.at[m], r4_sem.at[m], z_peer(step)
            )

    def await_given_near(m):
        wait_for(recv_s.at[m], r4_sem.at[m])

    def finish(m):
        for k in range(N_K):
            top = 32 * (k % 2)
            for c in range(N_C):
                col = HALF * (k // 2) + 128 * c
                if col < D:
                    gtok_ref[m, top : top + 32, col : col + 128] = fin[m, k, c]
        ids = ids_ref[m]
        place_of = (D - HALF) // 128
        table = jnp.concatenate([fin[m, 2, place_of], fin[m, 3, place_of]], axis=0).astype(F32).T
        gprob_ref[m] = jnp.concatenate(
            [
                jnp.sum(jnp.where(ids[k : k + 1] == expert_row, table, 0.0), axis=0, keepdims=True)
                for k in range(TOPK)
            ],
            axis=0,
        )

    for copy in input_copies[:4]:
        copy.wait()
    prepare(0)
    pl.semaphore_wait(barrier, greeted)
    send_forward(0)
    for copy in input_copies[4:]:
        copy.wait()
    prepare(1)
    wait_for(send_f.at[0], sf_sem.at[0])
    send_forward(1)
    for copy in weight_copies:
        copy.wait()

    wait_for(send_f.at[0], rf_sem.at[0])
    compute(0)
    send_back(0)
    wait_for(send_f.at[1], rf_sem.at[1])
    compute(1)
    send_back(1)
    wait_for(send_r.at[0], rr_sem.at[0])
    combine(0)
    send_near(0)

    acts = wact_buf[...].reshape(512, UNITS)
    for part in range(4):
        cols = slice(512 * part, 512 * (part + 1))
        gdown[:, cols] = lax.dot_general(
            acts, recv_f[:, :, :, cols].reshape(512, 512), (((0,), (0,)), ((), ())),
            preferred_element_type=F32,
        ).astype(BF16)
    out_copy = pltpu.make_async_copy(gdown, gdown_ref, out_sem)
    out_copy.start()

    await_near(0)
    send_kin(0)
    wait_for(send_r.at[1], rr_sem.at[1])
    combine(1)
    send_near(1)
    await_kin(0)
    give_kin(0)
    await_near(1)
    send_kin(1)
    await_given_kin(0)
    give_near(0)
    await_kin(1)
    give_kin(1)
    await_given_near(0)
    finish(0)
    await_given_kin(1)
    give_near(1)
    await_given_near(1)
    finish(1)
    out_copy.wait()
    wait_for(send_f.at[1], sf_sem.at[1])
    for m in range(MICRO):
        wait_for(send_r.at[m], sr_sem.at[m])
        wait_for(recv_s.at[m], s1_sem.at[m])
        wait_but_own(recv_w.at[m], s2_sem.at[m])

        @pl.when(owner)
        def _():
            wait_for(recv_w.at[m], s3_sem.at[m])

        wait_for(recv_s.at[m], s4_sem.at[m])


def body(tokens, cotangent, expert_ids, route_probs, gate_weight, up_weight, down_weight):
    vmem = pl.BlockSpec(memory_space=pltpu.VMEM)
    hbm = pl.BlockSpec(memory_space=pltpu.HBM)
    gtok, gprob, gdown = pl.pallas_call(
        kernel,
        name="expert_backward",
        out_shape=(
            jax.ShapeDtypeStruct((MICRO, TOK, D), BF16),
            jax.ShapeDtypeStruct((MICRO, TOPK, TOK), F32),
            jax.ShapeDtypeStruct((UNITS, D), BF16),
        ),
        in_specs=[hbm] * 7,
        out_specs=(vmem, vmem, pl.BlockSpec(memory_space=pl.ANY)),
        scratch_shapes=[
            pltpu.VMEM((MICRO, 2 * TOK, D), BF16),
            pltpu.VMEM((MICRO, TOPK, TOK), jnp.int32),
            pltpu.VMEM((MICRO, TOPK, TOK), BF16),
            pltpu.VMEM((3 * UNITS, D), BF16),
            pltpu.VMEM((MICRO, 256, 128), BF16),
            pltpu.VMEM((MICRO, 15, 16, WIDE), BF16),
            pltpu.VMEM((MICRO, 16, 16, WIDE), BF16),
            pltpu.VMEM((MICRO, 15, 16, HALF), BF16),
            pltpu.VMEM((MICRO, 16, 16, HALF), BF16),
            pltpu.VMEM((MICRO, N_K, N_C, *CHUNK), BF16),
            pltpu.VMEM((MICRO, 3, N_C, *CHUNK), BF16),
            pltpu.VMEM((MICRO, N_C, *CHUNK), BF16),
            pltpu.VMEM((MICRO, N_T * N_Y - 1, *CHUNK), BF16),
            pltpu.VMEM((MICRO, N_K, N_C, *CHUNK), BF16),
            pltpu.VMEM((UNITS, D), BF16),
            pltpu.VMEM((MICRO, 256, UNITS), BF16),
            pltpu.SemaphoreType.DMA((6,)),
            pltpu.SemaphoreType.DMA((3,)),
            pltpu.SemaphoreType.DMA,
        ] + [pltpu.SemaphoreType.DMA((MICRO,))] * 12,
        compiler_params=pltpu.CompilerParams(
            collective_id=0, has_side_effects=True, vmem_limit_bytes=60 << 20
        ),
    )(
        tokens, cotangent,
        jnp.transpose(expert_ids, (0, 2, 1)), jnp.transpose(route_probs, (0, 2, 1)),
        gate_weight[0], up_weight[0], down_weight[0],
    )
    return gtok, jnp.transpose(gprob, (0, 2, 1)), gdown[None]


def solution(mesh):
    return jax.shard_map(
        body,
        mesh=mesh,
        in_specs=(
            P(None, "exp", None),
            P(None, "exp", None),
            P(None, "exp", None),
            P(None, "exp", None),
            P("exp", "rep", None),
            P("exp", "rep", None),
            P("exp", "rep", None),
        ),
        out_specs=(P(None, "exp", None), P(None, "exp", None), P("exp", "rep", None)),
        check_vma=False,
    )
```

```python
import jax
import jax.numpy as jnp
from jax import lax
from jax.experimental import pallas as pl
from jax.experimental.pallas import tpu as pltpu
from jax.sharding import PartitionSpec as P

MESH = pl.DeviceIdType.MESH
FF = 1536
TOPK = 8
EXPERTS = 128
MICRO = 2
CAP = 8
N_EXP = 16
N_Z = 12
N_Y = 4
N_K = 4
N_T = N_Z // N_K
N_C = 9
N_OWN = N_C // N_T
PER_GROUP = EXPERTS // N_EXP
TOK = 64
D = 2048
UNITS = 256
WIDE = D + 128
HALF = 1152
CHUNK = (32, 128)
BF16 = jnp.bfloat16
F32 = jnp.float32


def flip(a, d):
    out = 0
    for bit in (1, 2, 4, 8):
        out = out + ((a // bit + d // bit) % 2) * bit
    return out


def kernel(
    tok_hbm, cot_hbm, ids_hbm, probs_hbm, gate_hbm, up_hbm, down_hbm,
    gtok_ref, gprob_ref, gdown_ref,
    rows_ref, ids_ref, probs_ref, weights, pick, send_f, recv_f, send_r, recv_r,
    red, recv_s, part_z, recv_w, fin, gdown, wact_buf,
    in_sem, w_sem, out_sem,
    sf_sem, rf_sem, sr_sem, rr_sem, s1_sem, r1_sem, s2_sem, r2_sem,
    s3_sem, r3_sem, s4_sem, r4_sem,
):
    rep = lax.axis_index("rep")
    me = lax.axis_index("exp")
    z = rep // N_Y
    y_hi = rep % N_Y
    y_lo = me // 8
    core = me % 2
    kind = z % N_K
    turn = z // N_K

    def local_expert(r):
        return r * UNITS // FF

    def far_side(m, d):
        return (d // 8) * ((d + m) % 2)

    def rep_of(m, d):
        step = far_side(m, d) * (2 * y_lo - 1)
        return z * N_Y + (y_hi + step + N_Y) % N_Y

    def exp_peer(m, p):
        d = p + 1
        return (rep_of(m, d), flip(me, d))

    def z_peer(step):
        return (((z + step + N_Z) % N_Z) * N_Y + y_hi, me)

    def kin(q):
        to_turn, to_y = (turn + q // N_Y) % N_T, (y_hi + q) % N_Y
        return ((to_turn * N_K + kind) * N_Y + to_y, me), to_turn * N_OWN + to_y, to_y < N_OWN

    input_copies = [
        pltpu.make_async_copy(src, dst, in_sem.at[i])
        for i, (src, dst) in enumerate((
            (ids_hbm, ids_ref),
            (probs_hbm, probs_ref),
            (tok_hbm.at[0], rows_ref.at[0, pl.ds(0, TOK)]),
            (cot_hbm.at[0], rows_ref.at[0, pl.ds(TOK, TOK)]),
            (tok_hbm.at[1], rows_ref.at[1, pl.ds(0, TOK)]),
            (cot_hbm.at[1], rows_ref.at[1, pl.ds(TOK, TOK)]),
        ))
    ]
    weight_copies = [
        pltpu.make_async_copy(src, weights.at[pl.ds(UNITS * i, UNITS)], w_sem.at[i])
        for i, src in enumerate((gate_hbm, up_hbm, down_hbm))
    ]
    for copy in input_copies:
        copy.start()
    for copy in weight_copies:
        copy.start()

    barrier = pltpu.get_barrier_semaphore()

    def greet(device):
        pl.semaphore_signal(barrier, inc=1, device_id=device, device_id_type=MESH)

    @pl.loop(0, N_EXP - 1)
    def _(p):
        greet(exp_peer(0, p))

    @pl.loop(7, N_EXP - 1)
    def _(p):
        greet(exp_peer(1, p))

    for step in (1, -1, 2, -2):
        greet(z_peer(step))

    @pl.loop(1, N_T * N_Y)
    def _(q):
        greet(kin(q)[0])

    greeted = (N_EXP - 1) + 8 + 4 + (N_T * N_Y - 1)

    row = lax.broadcasted_iota(jnp.int32, (256, 1), 0)
    row_d = (row // 16 + 1) % 16
    row_half = (row // 8) % 2
    row_slot = (row % 8).astype(F32)
    row_exp = flip(me, row_d)
    expert_lane = lax.broadcasted_iota(jnp.int32, (1, EXPERTS), 1)
    expert_row = lax.broadcasted_iota(jnp.int32, (EXPERTS, 1), 0)
    earlier = (
        lax.broadcasted_iota(jnp.int32, (TOK, TOK), 0)
        < lax.broadcasted_iota(jnp.int32, (TOK, TOK), 1)
    ).astype(BF16)

    def prepare(m):
        ids = ids_ref[m]
        probs = probs_ref[m].astype(F32)
        near, far = local_expert(rep), local_expert(rep_of(m, 9 - m))
        group = near + far_side(m, row_d) * (far - near)
        row_expert = row_exp * PER_GROUP + group
        member = jnp.zeros((256, TOK), F32)
        table = jnp.zeros((EXPERTS, TOK), F32)
        for k in range(TOPK):
            route = ids[k : k + 1]
            member = member + jnp.where(route == row_expert, 1.0, 0.0)
            table = table + jnp.where(route == expert_row, probs[k : k + 1], 0.0)
        before = jnp.dot(member.astype(BF16), earlier, preferred_element_type=F32)
        one_hot = jnp.where(before == row_slot, member, 0.0)
        first = jnp.where(row_half == 0, one_hot, 0.0)
        second = jnp.where(row_half == 1, one_hot, 0.0)
        chosen = jnp.concatenate([first, second], axis=1).astype(BF16)
        pick[m] = chosen

        def put(start, size, out):
            out = out.astype(BF16).reshape(16, 16, size)
            send_f[m, :, :, start : start + size] = out[:15]
            recv_f[m, 15, :, start : start + size] = out[15]

        for start in (0, 1024):
            put(start, 1024, jnp.dot(
                chosen, rows_ref[m, :, start : start + 1024], preferred_element_type=F32
            ))
        put(D, 128, lax.dot_general(
            one_hot.astype(BF16), table.astype(BF16), (((1,), (1,)), ((), ())),
            preferred_element_type=F32,
        ))

    def start_all(count, src, dst, send_sem, recv_sem, peer):
        @pl.loop(0, count)
        def _(i):
            pltpu.make_async_remote_copy(
                src_ref=src(i), dst_ref=dst(i), send_sem=send_sem, recv_sem=recv_sem,
                device_id=peer(i), device_id_type=MESH,
            ).start()

    def wait_for(ref, sem):
        pltpu.make_async_copy(ref, ref, sem).wait()

    def place(i):
        return ((5 + 6 * core) * (i + 1)) % N_EXP - 1

    def send_forward(m):
        start_all(
            15, lambda i: send_f.at[m, place(i)], lambda i: recv_f.at[m, place(i)],
            sf_sem.at[m], rf_sem.at[m], lambda i: exp_peer(m, place(i)),
        )

    def compute(m):
        rows = recv_f[m].reshape(256, WIDE)
        pre = lax.dot_general(
            rows[:, :D], weights[...], (((1,), (1,)), ((), ())), preferred_element_type=F32
        ).reshape(16, 2, 8, 3 * UNITS)
        gate_pre = pre[:, 0, :, :UNITS].reshape(128, UNITS)
        up_pre = pre[:, 0, :, UNITS : 2 * UNITS].reshape(128, UNITS)
        act_grad = pre[:, 1, :, 2 * UNITS :].reshape(128, UNITS)
        mine = (expert_lane == me * PER_GROUP + local_expert(rep)).astype(F32)
        prob = rows[:, D:].astype(F32).reshape(16, 2, 8, 128)[:, 0].reshape(128, 128)
        prob = jnp.sum(prob * mine, axis=1, keepdims=True)
        sigmoid_gate = jax.nn.sigmoid(gate_pre)
        silu_gate = gate_pre * sigmoid_gate
        act = silu_gate * up_pre
        prob_part = jnp.sum(act * act_grad, axis=1, keepdims=True)
        wact = (prob * act).reshape(16, 1, 8, UNITS)
        scaled = prob * act_grad
        gate_grad = scaled * up_pre * sigmoid_gate * (1.0 + gate_pre * (1.0 - sigmoid_gate))
        up_grad = scaled * silu_gate
        wact_buf[m] = (
            jnp.concatenate([jnp.zeros_like(wact), wact], axis=1).reshape(256, UNITS).astype(BF16)
        )
        grads = jnp.concatenate([gate_grad, up_grad], axis=1).astype(BF16)
        left = jnp.dot(grads, weights[: 2 * UNITS, :HALF], preferred_element_type=F32)
        right = jnp.dot(grads, weights[: 2 * UNITS, HALF:], preferred_element_type=F32)
        right = jnp.concatenate([right, prob_part * mine, jnp.zeros((128, 128), F32)], axis=1)
        out = jnp.concatenate(
            [left.reshape(16, 8, HALF), right.reshape(16, 8, HALF)], axis=1
        ).astype(BF16)
        send_r[m] = out[:15]
        recv_r[m, 15] = out[15]

    def send_back(m):
        start_all(
            15, lambda i: send_r.at[m, place(i)], lambda i: recv_r.at[m, place(i)],
            sr_sem.at[m], rr_sem.at[m], lambda i: exp_peer(m, place(i)),
        )

    def combine(m):
        total = lax.dot_general(
            pick[m], recv_r[m].reshape(256, HALF), (((0,), (0,)), ((), ())),
            preferred_element_type=F32,
        ).astype(BF16)
        for k in range(N_K):
            for c in range(N_C):
                red[m, k, c] = total[32 * k : 32 * (k + 1), 128 * c : 128 * (c + 1)]

    def start_one(src, dst, send_sem, recv_sem, device):
        pltpu.make_async_remote_copy(
            src_ref=src, dst_ref=dst, send_sem=send_sem, recv_sem=recv_sem,
            device_id=device, device_id_type=MESH,
        ).start()

    low, high = pl.ds(0, 5), pl.ds(5, N_C - 5)
    owner = y_hi < N_OWN
    own = turn * N_OWN + y_hi

    def send_near(m):
        across = (kind + 2) % N_K
        for step, part in ((2, low), (-2, high)):
            start_one(
                red.at[m, across, part], recv_s.at[m, 2, part],
                s1_sem.at[m], r1_sem.at[m], z_peer(step),
            )
        for slot, step in enumerate((1, -1)):
            start_one(
                red.at[m, (kind + step + N_K) % N_K], recv_s.at[m, slot],
                s1_sem.at[m], r1_sem.at[m], z_peer(step),
            )

    def await_near(m):
        wait_for(recv_s.at[m], r1_sem.at[m])
        total = red[m, kind].astype(F32)
        for slot in range(3):
            total = total + recv_s[m, slot].astype(F32)
        part_z[m] = total.astype(BF16)

    def send_kin(m):
        @pl.loop(0, N_T * N_Y - 1)
        def _(i):
            q = (i + 5) % (N_T * N_Y - 1) + 1
            device, chunk, owns = kin(q)

            @pl.when(owns)
            def _():
                start_one(
                    part_z.at[m, chunk], recv_w.at[m, q - 1], s2_sem.at[m], r2_sem.at[m], device
                )

    def await_kin(m):
        @pl.when(owner)
        def _():
            wait_for(recv_w.at[m], r2_sem.at[m])
            total = part_z[m, own].astype(F32)
            for slot in range(N_T * N_Y - 1):
                total = total + recv_w[m, slot].astype(F32)
            fin[m, kind, own] = total.astype(BF16)

    def give_kin(m):
        @pl.when(owner)
        def _():
            @pl.loop(0, N_T * N_Y - 1)
            def _(i):
                q = (i + 5) % (N_T * N_Y - 1) + 1
                start_one(
                    fin.at[m, kind, own], fin.at[m, kind, own],
                    s3_sem.at[m], r3_sem.at[m], kin(q)[0],
                )

    def wait_but_own(ref, sem):
        @pl.when(owner)
        def _():
            wait_for(ref.at[pl.ds(0, N_C - 1)], sem)

        @pl.when(jnp.logical_not(owner))
        def _():
            wait_for(ref.at[pl.ds(0, N_C)], sem)

    def await_given_kin(m):
        wait_but_own(recv_w.at[m], r3_sem.at[m])

    def give_near(m):
        for step, part in ((2, low), (-2, high)):
            start_one(
                fin.at[m, kind, part], fin.at[m, kind, part],
                s4_sem.at[m], r4_sem.at[m], z_peer(step),
            )
        for step in (1, -1):
            start_one(
                fin.at[m, kind], fin.at[m, kind], s4_sem.at[m], r4_sem.at[m], z_peer(step)
            )

    def await_given_near(m):
        wait_for(recv_s.at[m], r4_sem.at[m])

    def finish(m):
        for k in range(N_K):
            top = 32 * (k % 2)
            for c in range(N_C):
                col = HALF * (k // 2) + 128 * c
                if col < D:
                    gtok_ref[m, top : top + 32, col : col + 128] = fin[m, k, c]
        ids = ids_ref[m]
        place_of = (D - HALF) // 128
        table = jnp.concatenate([fin[m, 2, place_of], fin[m, 3, place_of]], axis=0).astype(F32).T
        gprob_ref[m] = jnp.concatenate(
            [
                jnp.sum(jnp.where(ids[k : k + 1] == expert_row, table, 0.0), axis=0, keepdims=True)
                for k in range(TOPK)
            ],
            axis=0,
        )

    for copy in input_copies[:4]:
        copy.wait()
    prepare(0)
    pl.semaphore_wait(barrier, greeted)
    send_forward(0)
    for copy in input_copies[4:]:
        copy.wait()
    prepare(1)
    wait_for(send_f.at[0], sf_sem.at[0])
    send_forward(1)
    for copy in weight_copies:
        copy.wait()

    wait_for(send_f.at[0], rf_sem.at[0])
    compute(0)
    send_back(0)
    wait_for(send_f.at[1], rf_sem.at[1])
    compute(1)
    send_back(1)
    wait_for(send_r.at[0], rr_sem.at[0])
    combine(0)
    send_near(0)

    acts = wact_buf[...].reshape(512, UNITS)
    for part in range(4):
        cols = slice(512 * part, 512 * (part + 1))
        gdown[:, cols] = lax.dot_general(
            acts, recv_f[:, :, :, cols].reshape(512, 512), (((0,), (0,)), ((), ())),
            preferred_element_type=F32,
        ).astype(BF16)
    out_copy = pltpu.make_async_copy(gdown, gdown_ref, out_sem)
    out_copy.start()

    await_near(0)
    send_kin(0)
    wait_for(send_r.at[1], rr_sem.at[1])
    combine(1)
    send_near(1)
    await_kin(0)
    give_kin(0)
    await_near(1)
    send_kin(1)
    await_given_kin(0)
    give_near(0)
    await_kin(1)
    give_kin(1)
    await_given_near(0)
    finish(0)
    await_given_kin(1)
    give_near(1)
    await_given_near(1)
    finish(1)
    out_copy.wait()
    wait_for(send_f.at[1], sf_sem.at[1])
    for m in range(MICRO):
        wait_for(send_r.at[m], sr_sem.at[m])
        wait_for(recv_s.at[m], s1_sem.at[m])
        wait_but_own(recv_w.at[m], s2_sem.at[m])

        @pl.when(owner)
        def _():
            wait_for(recv_w.at[m], s3_sem.at[m])

        wait_for(recv_s.at[m], s4_sem.at[m])


def hand_on_kernel(*refs):
    sources, results, sem = refs[:3], refs[3:6], refs[6]
    copies = []
    for source, result in zip(sources, results):
        rows = source.shape[0]
        pieces = 4 if rows == UNITS else rows
        for p in range(pieces):
            part = pl.ds(p * (rows // pieces), rows // pieces)
            copies.append(
                pltpu.make_async_copy(source.at[part], result.at[part], sem.at[len(copies)])
            )
    for copy in copies:
        copy.start()
    for copy in copies:
        copy.wait()


def hand_on(*arrays):
    anywhere = pl.BlockSpec(memory_space=pl.ANY)
    return pl.pallas_call(
        hand_on_kernel,
        name="hand_on",
        out_shape=tuple(jax.ShapeDtypeStruct(a.shape, a.dtype) for a in arrays),
        in_specs=[anywhere] * 3,
        out_specs=(anywhere,) * 3,
        scratch_shapes=[pltpu.SemaphoreType.DMA((8,))],
    )(*arrays)


def body(tokens, cotangent, expert_ids, route_probs, gate_weight, up_weight, down_weight):
    vmem = pl.BlockSpec(memory_space=pltpu.VMEM)
    hbm = pl.BlockSpec(memory_space=pltpu.HBM)
    gtok, gprob, gdown = pl.pallas_call(
        kernel,
        name="expert_backward",
        out_shape=(
            jax.ShapeDtypeStruct((MICRO, TOK, D), BF16),
            jax.ShapeDtypeStruct((MICRO, TOPK, TOK), F32),
            jax.ShapeDtypeStruct((UNITS, D), BF16),
        ),
        in_specs=[hbm] * 7,
        out_specs=(vmem, vmem, pl.BlockSpec(memory_space=pl.ANY)),
        scratch_shapes=[
            pltpu.VMEM((MICRO, 2 * TOK, D), BF16),
            pltpu.VMEM((MICRO, TOPK, TOK), jnp.int32),
            pltpu.VMEM((MICRO, TOPK, TOK), BF16),
            pltpu.VMEM((3 * UNITS, D), BF16),
            pltpu.VMEM((MICRO, 256, 128), BF16),
            pltpu.VMEM((MICRO, 15, 16, WIDE), BF16),
            pltpu.VMEM((MICRO, 16, 16, WIDE), BF16),
            pltpu.VMEM((MICRO, 15, 16, HALF), BF16),
            pltpu.VMEM((MICRO, 16, 16, HALF), BF16),
            pltpu.VMEM((MICRO, N_K, N_C, *CHUNK), BF16),
            pltpu.VMEM((MICRO, 3, N_C, *CHUNK), BF16),
            pltpu.VMEM((MICRO, N_C, *CHUNK), BF16),
            pltpu.VMEM((MICRO, N_T * N_Y - 1, *CHUNK), BF16),
            pltpu.VMEM((MICRO, N_K, N_C, *CHUNK), BF16),
            pltpu.VMEM((UNITS, D), BF16),
            pltpu.VMEM((MICRO, 256, UNITS), BF16),
            pltpu.SemaphoreType.DMA((6,)),
            pltpu.SemaphoreType.DMA((3,)),
            pltpu.SemaphoreType.DMA,
        ] + [pltpu.SemaphoreType.DMA((MICRO,))] * 12,
        compiler_params=pltpu.CompilerParams(
            collective_id=0, has_side_effects=True, vmem_limit_bytes=60 << 20
        ),
    )(
        tokens, cotangent,
        jnp.transpose(expert_ids, (0, 2, 1)), jnp.transpose(route_probs, (0, 2, 1)),
        gate_weight[0], up_weight[0], down_weight[0],
    )
    gtok, gprob, gdown = hand_on(gtok, gprob, gdown)
    return gtok, jnp.transpose(gprob, (0, 2, 1)), gdown[None]


def solution(mesh):
    return jax.shard_map(
        body,
        mesh=mesh,
        in_specs=(
            P(None, "exp", None),
            P(None, "exp", None),
            P(None, "exp", None),
            P(None, "exp", None),
            P("exp", "rep", None),
            P("exp", "rep", None),
            P("exp", "rep", None),
        ),
        out_specs=(P(None, "exp", None), P(None, "exp", None), P("exp", "rep", None)),
        check_vma=False,
    )
```
